512 devices in a mesh: dp: 32 (over z_lo, y), vocab: 16 (over z_hi, x, core).
Axes of the slice: x: 4, y: 8, z: 8 (z_hi: 2, z_lo: 4; z = z_hi * 4 + z_lo), core: 2. Of those that a mesh axis runs over, the one named last changes fastest.
Arguments:
- hidden_states: bfloat16 [4096, 5120], P('dp'), may hold values from -16 to 16
- positions: int32 [64, 16], P('dp'), may hold values from 0 to 127
- target_ids: int32 [64, 16], replicated, may hold values from 0 to 151551
- head: bfloat16 [151552, 5120], P(('dp', 'vocab')), may hold values from -3 to 3
- out_factor: bfloat16 [151552, 128], P(('dp', 'vocab')), may hold values from -0.5 to 0.5
- in_factor: bfloat16 [5120, 128], P('vocab'), may hold values from -0.0048828125 to 0.0048828125
Outputs:
- gram: float32 [64, 64], P('dp', 'vocab')
The draws below stay inside these ranges and needn't reach their ends.
All inputs are finite; a program needn't handle non-finite values.
Results may differ from the reference program's by a relative error of at most 0.00078.
Values may be sent and summed in bfloat16 or wider, within the bound.
A program may use at most 64 MiB of HBM per device.

```python
import math
import jax
import jax.numpy as jnp
import numpy as np
from jax import lax

D = 5120
R = 128
TPE = 16
SEL = 2
SEQ_DEV = 128
VOCAB = 151552
EX = 64
ROWS_ALL = 4096
N_DP = 32


def head_row(key, index):
    row_key = jax.random.fold_in(jax.random.fold_in(key, 11), index)
    values = jnp.clip(jax.random.normal(row_key, (D,), jnp.float32), -6.0, 6.0)
    return values * (3.0 / math.sqrt(D))


def draw_head(key, part):
    indices = jnp.arange(VOCAB, dtype=jnp.int32)
    return jax.vmap(lambda index: head_row(key, index))(indices).astype(jnp.bfloat16)


def draw_hidden_states(key, part):
    own_key = jax.random.fold_in(key, 3)
    values = jnp.clip(jax.random.normal(own_key, (ROWS_ALL, D), jnp.float32), -6.0, 6.0)
    return values.astype(jnp.bfloat16)


def place_ends(drawn, key, smallest, largest):
    extent = drawn.shape
    place = [jax.random.randint(jax.random.fold_in(key, axis), (), 0, extent[axis]) for axis in range(len(extent))]
    drawn = drawn.at[tuple(place)].set(smallest)
    longest = extent.index(max(extent))
    place[longest] = (place[longest] + 1) % extent[longest]
    return drawn.at[tuple(place)].set(largest)


def block_levels(stream_key, dims, cuts, least, top_value):
    factor_of, own = 1.0, jax.random.fold_in(stream_key, 6)
    for position, blocks in cuts:
        heights = jnp.exp(jax.random.uniform(jax.random.fold_in(own, position), (blocks,), jnp.float32, least / len(cuts), top_value / len(cuts)))
        factor_of = factor_of * jnp.repeat(heights, dims[position] // blocks).reshape([-1 if axis == position else 1 for axis in range(len(dims))])
    return factor_of


def wide_ids(key, dims, number_of, lean):
    weights = [min(1 << octave, number_of + 1 - (1 << octave)) * (1 << 20) // math.isqrt((1 << octave) ** lean) + 1 for octave in range((number_of + 1).bit_length()) if 1 << octave <= number_of]
    spread = 1 + sum(weights) // (1 << 30)
    table = np.cumsum(np.array([max(1, weight // spread) for weight in weights]))
    ticket = jax.random.randint(jax.random.fold_in(key, 1), dims, 0, int(table[len(weights) - 1]))
    start = jnp.left_shift(1, jnp.searchsorted(jnp.asarray(table, jnp.int32), ticket, side="right").astype(jnp.int32))
    grade = start - 1 + jax.random.randint(jax.random.fold_in(key, 4), dims, 0, 1 << 30) % jnp.minimum(start, number_of + 1 - start)
    return jax.random.permutation(jax.random.fold_in(key, 2), number_of)[grade].astype(jnp.int32)


def centred(rng, extent, spread, reach, shards=(), kind=jnp.bfloat16):
    drawn = spread * jax.random.normal(rng, extent, jnp.float32)
    if shards:
        drawn = drawn * block_levels(rng, extent, shards, -0.22, 0.18)
    return jnp.clip(drawn, -reach, reach).astype(kind)


def setup_inputs(seed: int = 0) -> dict:
    key_of = jax.random.split(jax.random.key(seed), 7)
    hidden_states = draw_hidden_states(jax.random.fold_in(key_of[6], 71), 0)
    positions = place_ends(jax.random.randint(key_of[1], (EX, TPE), 0, SEQ_DEV), jax.random.fold_in(key_of[1], 1), 0, SEQ_DEV - 1).astype(jnp.int32)
    target_ids = place_ends(wide_ids(key_of[2], (EX, TPE), VOCAB, 2), jax.random.fold_in(key_of[2], 3), 0, VOCAB - 1).astype(jnp.int32)
    head = draw_head(jax.random.fold_in(key_of[6], 71), 0)
    out_factor = centred(key_of[4], (VOCAB, R), R ** -0.5, 0.5, ((0, 512),))
    in_factor = centred(key_of[5], (D, R), (D * 16 * TPE) ** -0.5, 0.0048828125, ((0, 16),))
    return {"hidden_states": hidden_states, "positions": positions, "target_ids": target_ids, "head": head, "out_factor": out_factor, "in_factor": in_factor}


entropy_weight = 0.2


def reference(hidden_states, positions, target_ids, head, out_factor, in_factor):
    grouped = hidden_states.reshape(N_DP, SEQ_DEV, D)
    where_rows = positions.reshape(N_DP, SEL * TPE).astype(jnp.int32)
    selected = jnp.take_along_axis(grouped, where_rows[:, :, None], axis=1)
    targets = target_ids.reshape(N_DP, SEL * TPE).astype(jnp.int32)

    def group_grads(inputs):
        rows_here, targets_here = inputs
        logits = jnp.dot(rows_here, head.T, preferred_element_type=jnp.float32)
        row_max = jnp.max(logits, axis=1)
        shifted = jnp.exp(logits - row_max[:, None])
        exp_total = jnp.sum(shifted, axis=1)
        weighted = jnp.sum(shifted * logits, axis=1)
        log_total = row_max + jnp.log(exp_total)
        entropy = log_total - weighted / exp_total
        probs = jnp.exp(logits - log_total[:, None])
        vocab_ids = lax.broadcasted_iota(jnp.int32, logits.shape, 1)
        hits = (vocab_ids == targets_here[:, None]).astype(logits.dtype)
        grads = probs - hits + entropy_weight * probs * (logits - log_total[:, None] + entropy[:, None])
        return jnp.dot(grads.astype(jnp.bfloat16), out_factor, preferred_element_type=jnp.float32)

    out_side = lax.map(group_grads, (selected, targets)).reshape(EX, TPE, R)
    flat_rows = selected.reshape(EX * TPE, D)
    input_side = jnp.dot(flat_rows, in_factor, preferred_element_type=jnp.float32).reshape(EX, TPE, R)
    features = jnp.einsum("etr,etc->erc", out_side, input_side, precision=lax.Precision.HIGHEST)
    features = features.reshape(EX, R * R).astype(jnp.bfloat16)
    return jnp.dot(features, features.T, preferred_element_type=jnp.float32)
```

```python
import jax
import jax.numpy as jnp
from jax import lax
from jax.experimental import pallas as pl
from jax.experimental.pallas import tpu as pltpu
from jax.sharding import PartitionSpec as P

entropy_weight = 0.2
MESH = pl.DeviceIdType.MESH
NX, NY, NZ, NL = 4, 8, 8, 4
F32, BF16 = jnp.float32, jnp.bfloat16
NT = (((1,), (1,)), ((), ()))
TN = (((0,), (0,)), ((), ()))

DIRECT, QUARTER = 1536, 512
WIDE = 2 * DIRECT + QUARTER
HALF_RECT = WIDE // 2
PIECE = HALF_RECT // 2


def device(x, y, z, c):
    return (lax.rem(z, NL) * NY + y, (z // NL) * 2 * NX + x * 2 + c)


def kernel(
    hidden, positions, targets, head, out_factor, in_factor, gram,
    sel, onehot, in_pad, logits, stats, stats_in, proj, core_in, by_rank, x_in, by_y, y_in, own, z_in,
    side, side_in, side_cols, out_own, out_rows, out_cols,
    s_y, s_z, t_z, t_y, x_s, sib_s, st_s, pc_s, px_s, py_s, pz_s, is_s, ix_s, iz_s, id_s, row_s, row_send, col_s, col_send,
):
    dp, v = lax.axis_index("dp"), lax.axis_index("vocab")
    y, zl = lax.rem(dp, NY), dp // NY
    zh, x, c = v // (2 * NX), lax.rem(v, 2 * NX) // 2, lax.rem(v, 2)
    z = zh * NL + zl
    voc_local = head.shape[0]

    def at(dx=0, dy=0, dz=0, dc=0):
        return device(
            lax.rem(x + dx + NX, NX), lax.rem(y + dy + NY, NY), lax.rem(z + dz + NZ, NZ), lax.rem(c + dc, 2)
        )

    x_line = [(dx, dc) for dx in range(NX) for dc in range(2) if dx or dc]
    pending = []

    def copy(src, dst, sent, received, to):
        return pltpu.make_async_remote_copy(
            src_ref=src, dst_ref=dst, send_sem=sent, recv_sem=received, device_id=to, device_id_type=MESH
        )

    def send(src, dst, sems, index, to):
        made = copy(src, dst, sems.at[0, index], sems.at[1, index], to)
        made.start()
        pending.append(made)

    def arrive(dst, sems, index):
        copy(dst, dst, sems.at[0, index], sems.at[1, index], at(dc=1)).wait_recv()

    gives_rows = zl == x
    gives_cols = zh == x // 2
    col_x, col_c = 2 * lax.rem(x, 2) + y // 4, lax.rem(y, 4) // 2
    from_x = zh * 2 + x // 2

    def from_y(i):
        return lax.rem(x, 2) * 4 + c * 2 + i

    own_col = jnp.logical_and(col_x == x, col_c == c)

    barrier = pltpu.get_barrier_semaphore()

    def greet(to):
        pl.semaphore_signal(barrier, inc=1, device_id=to, device_id_type=MESH)

    for dx, dc in x_line:
        greet(at(dx=dx, dc=dc))
    for d in range(1, NY):
        greet(at(dy=d))
        greet(at(dz=d))
    for i in range(2):
        @pl.when(2 * v + i != dp)
        def _():
            greet((2 * v + i, dp // 2))
        for e in range(2):
            @pl.when(jnp.logical_not((from_x == x) & (from_y(i) == y) & (c == e)))
            def _():
                greet(device(from_x, from_y(i), z, e))
    expected = 21 + 2 - (dp // 2 == v).astype(jnp.int32)
    expected += jnp.where(gives_cols, 8 - own_col.astype(jnp.int32), 0)

    place = jnp.concatenate(
        [positions[0:1, :], positions[1:2, :], jnp.full((1, 96), -1, jnp.int32)], axis=1
    )
    hot = (lax.broadcasted_iota(jnp.int32, (128, 128), 0) == place).astype(F32)
    onehot[...] = jnp.transpose(hot)[0:32].astype(BF16)
    mine = onehot[pl.ds(pl.multiple_of(c * 16, 16), 16), :]

    def quarter_of(d):
        return 2 * DIRECT + QUARTER * lax.rem(x - d + NX, NX)

    def whole_column(j):
        j = jnp.asarray(j, jnp.int32)
        start = jnp.where(
            j < 3, j * 512, jnp.where(j == 3, quarter_of(0), jnp.where(j < 7, j * 512 - 512, quarter_of(j - 6)))
        )
        return pl.ds(pl.multiple_of(start, 512), 512)

    for j in range(7):
        sel[c, y, zl, :, 512 * j : 512 * j + 512] = jnp.dot(
            mine, hidden[:, whole_column(j)], preferred_element_type=F32
        ).astype(BF16)

    pl.semaphore_wait(barrier, expected)

    def group(dy):
        return lax.rem(y + dy + NY, NY)

    def plane(dz):
        return lax.rem(zl + dz + NL, NL)

    def cols(start, size):
        return pl.ds(start, size)

    def s_piece(dy, dz, start=0, size=HALF_RECT):
        return sel.at[c, group(dy), plane(dz), :, cols(start, size)]

    def t_piece(dz, start=0, size=HALF_RECT):
        return sel.at[c, y, plane(dz), :, cols(HALF_RECT + start, size)]

    def t_block(dy, start=0, size=HALF_RECT):
        return sel.at[c, group(dy), :, :, cols(HALF_RECT + start, size)]

    def y_index(dy):
        return dy - 1 if dy > 0 else 3 - dy

    def y_part(dy):
        return (0, PIECE) if dy == -4 else (PIECE, PIECE) if dy == 4 else (0, HALF_RECT)

    def forward(k, block, sems):
        if k < 4:
            for dy, step in ((-k, 1), (k, -1)):
                part = y_part(dy - step)
                send(block(dy, *part), block(dy, *part), sems, y_index(dy - step), at(dy=step))

    def s_block(dy, start=0, size=HALF_RECT):
        return s_piece(dy, 0, start, size)

    def arrived(k, block, sems):
        for dy in (-k, k):
            arrive(block(dy, *y_part(dy)), sems, y_index(dy))

    z_moves = ((1, 0, HALF_RECT), (-1, 0, HALF_RECT), (2, 0, PIECE), (-2, PIECE, PIECE))

    def s_z_sends(dy):
        for n, (dz, start, size) in enumerate(z_moves):
            send(s_piece(dy, 0, start, size), s_piece(dy, 0, start, size), s_z, 4 * (dy % 8) + n, at(dz=dz))

    def s_z_arrive(dy):
        for n, (dz, start, size) in enumerate(z_moves):
            arrive(s_piece(dy, -dz, start, size), s_z, 4 * (dy % 8) + n)

    def pair(k):
        return (0,) if k == 0 else (4,) if k == 4 else (k, -k)

    def x_and_sibling(dy):
        for d in range(1, NX):
            send(
                sel.at[c, group(dy), :, :, cols(DIRECT, QUARTER)],
                sel.at[c, group(dy), :, :, cols(WIDE + QUARTER * (d - 1), QUARTER)],
                x_s, 3 * (dy % 8) + d - 1, at(dx=d),
            )
        block = sel.at[c, group(dy), :, :, cols(0, WIDE)]
        send(block, block, sib_s, 2 * (dy % 8), at(dc=1))

    def x_arrive(dy):
        for d in range(1, NX):
            arrive(sel.at[c, group(dy), :, :, cols(WIDE + QUARTER * (d - 1), QUARTER)], x_s, 3 * (dy % 8) + d - 1)
        block = sel.at[c, group(dy), :, :, cols(WIDE, 3 * QUARTER)]
        send(block, block, sib_s, 2 * (dy % 8) + 1, at(dc=1))

    def compute(k):
        dys = pair(k)
        for dy in dys:
            arrive(sel.at[1 - c, group(dy), :, :, cols(0, WIDE)], sib_s, 2 * (dy % 8))
            arrive(sel.at[1 - c, group(dy), :, :, cols(WIDE, 3 * QUARTER)], sib_s, 2 * (dy % 8) + 1)

        def part(j, total):
            where = pl.ds(pl.multiple_of(512 * j, 512), 512)
            rows = [
                sel[e, group(dy), :, :, where].reshape(64, 512) for dy in dys for e in range(2)
            ]
            return total + lax.dot_general(
                head[:, whole_column(j)], jnp.concatenate(rows, axis=0), NT, preferred_element_type=F32
            )

        total = lax.fori_loop(0, 10, part, jnp.zeros((voc_local, 128 * len(dys)), F32))
        for n, dy in enumerate(dys):
            values = total[:, 128 * n : 128 * n + 128]
            row = pl.ds(group(dy), 1)
            top = jnp.max(values, axis=0, keepdims=True)
            lowered = values - top
            power = jnp.exp(lowered)
            logits[group(dy)] = values
            stats[0, 0, row, :] = top
            stats[0, 1, row, :] = jnp.sum(power, axis=0, keepdims=True)
            stats[0, 2, row, :] = jnp.sum(power * lowered, axis=0, keepdims=True)

    def to_cols(i):
        there = lax.rem(dp, 2)
        return copy(side.at[3], side_cols.at[there], id_s.at[0, i], id_s.at[1, there], (2 * v + i, dp // 2))

    forward(0, s_block, s_y)
    for n, (dz, start, size) in enumerate(z_moves):
        send(t_piece(0, start, size), t_piece(0, start, size), t_z, n, at(dz=dz))
    s_z_sends(0)

    window = pl.multiple_of(v * 320 - 64 * c, 128)
    in_pad[...] = jnp.zeros_like(in_pad)
    in_pad[pl.ds(pl.multiple_of(64 * c, 64), 320), :] = in_factor[...]
    chosen = jnp.dot(onehot[...], hidden[:, pl.ds(window, 384)], preferred_element_type=F32).astype(BF16)
    side[0] = jnp.dot(chosen, in_pad[...], preferred_element_type=F32)
    send(side.at[0], side_in.at[0], is_s, 0, at(dc=1))

    for n, (dz, start, size) in enumerate(z_moves):
        arrive(t_piece(-dz, start, size), t_z, n)
    forward(0, t_block, t_y)

    arrive(side_in.at[0], is_s, 0)
    side[1] = side[0] + side_in[0]
    for d in range(1, NX):
        send(side.at[1], side_in.at[d], ix_s, d - 1, at(dx=d))

    for k in range(1, 5):
        arrived(k, s_block, s_y)
        forward(k, s_block, s_y)
        for dy in pair(k):
            s_z_sends(dy)
        for dy in pair(k - 1):
            s_z_arrive(dy)
            x_and_sibling(dy)
        if k == 1:
            for d in range(1, NX):
                arrive(side_in.at[d], ix_s, d - 1)
            side[2] = side[1] + side_in[1] + side_in[2] + side_in[3]
            send(side.at[2], side_in.at[4], iz_s, 0, at(dz=4))
        if k == 2:
            arrive(side_in.at[4], iz_s, 0)
            side[3] = side[2] + side_in[4]
            for i in range(2):
                @pl.when(2 * v + i == dp)
                def _():
                    side_cols[i] = side[3]

                @pl.when(2 * v + i != dp)
                def _():
                    to_cols(i).start()
        arrived(k, t_block, t_y)
        forward(k, t_block, t_y)
        if k >= 2:
            for dy in pair(k - 2):
                x_arrive(dy)
        if k >= 3:
            compute(k - 3)
    x_arrive(3)
    x_arrive(-3)
    s_z_arrive(4)
    x_and_sibling(4)
    compute(2)
    compute(3)
    x_arrive(4)
    compute(4)

    def merge(stage, peers):
        for n, to in enumerate(peers):
            send(stats.at[stage], stats_in.at[stage, n], st_s, 7 * stage + n, to)
        for n in range(7):
            arrive(stats_in.at[stage, n], st_s, 7 * stage + n)
        parts = [stats[stage]] + [stats_in[stage, n] for n in range(7)]
        top = parts[0][0]
        for part in parts[1:]:
            top = jnp.maximum(top, part[0])
        total, weighted = jnp.zeros_like(top), jnp.zeros_like(top)
        for part in parts:
            lower = part[0] - top
            scale = jnp.exp(lower)
            total += scale * part[1]
            weighted += scale * (part[2] + lower * part[1])
        stats[stage + 1, 0] = top
        stats[stage + 1, 1] = total
        stats[stage + 1, 2] = weighted

    merge(0, [at(dx=dx, dc=dc) for dx, dc in x_line])
    merge(1, [at(dy=d) for d in range(1, NY)])
    merge(2, [at(dz=d) for d in range(1, NZ)])
    log_sum = jnp.log(stats[3, 1])
    log_total = stats[3, 0] + log_sum
    entropy = log_sum - stats[3, 2] / stats[3, 1]

    wanted = jnp.concatenate(
        [targets[pl.ds(16 * b + e, 8, stride=2), :] for e in range(2) for b in range(NL)], axis=1
    )
    ids = lax.broadcasted_iota(jnp.int32, (voc_local, 128), 0) + (dp * 2 * NX * 2 + v) * voc_local
    for g in range(NY):
        lowered = logits[g] - log_total[g : g + 1, :]
        probs = jnp.exp(lowered)
        hits = (ids == wanted[g : g + 1, :]).astype(F32)
        grads = probs - hits + entropy_weight * probs * (lowered + entropy[g : g + 1, :])
        result = lax.dot_general(grads.astype(BF16), out_factor[...], TN, preferred_element_type=F32)
        proj[:, :, g] = result.reshape(2, NL, 16, 128)

    send(proj.at[1 - c], core_in, pc_s, 0, at(dc=1))
    arrive(core_in, pc_s, 0)
    by_rank[...] = proj[c] + core_in[...]
    for d in range(1, NX):
        send(by_rank.at[lax.rem(x + d, NX)], x_in.at[d - 1], px_s, d - 1, at(dx=d))
    for d in range(1, NX):
        arrive(x_in.at[d - 1], px_s, d - 1)
    by_y[...] = by_rank[x] + x_in[0] + x_in[1] + x_in[2]
    for d in range(1, NY):
        send(by_y.at[lax.rem(y + d, NY)], y_in.at[d - 1], py_s, d - 1, at(dy=d))
    for d in range(1, NY):
        arrive(y_in.at[d - 1], py_s, d - 1)
    own[...] = by_y[y] + jnp.sum(y_in[...], axis=0)
    for d in range(1, NZ):
        send(own, z_in.at[d - 1], pz_s, d - 1, at(dz=d))
    for d in range(1, NZ):
        arrive(z_in.at[d - 1], pz_s, d - 1)
    out_own[...] = own[...] + jnp.sum(z_in[...], axis=0)

    def row_copy(n):
        dx, dc = x_line[n]
        return copy(out_own, out_rows.at[c], row_send.at[n], row_s.at[c], at(dx=dx, dc=dc))

    slot = lax.rem(y, 2) * 2 + c

    def col_copy(d):
        to = device(col_x, lax.rem(y + d, NY), z, col_c)
        return copy(out_own, out_cols.at[slot], col_send.at[d], col_s.at[slot], to)

    @pl.when(gives_rows)
    def _():
        out_rows[c] = out_own[...]
        for n in range(7):
            row_copy(n).start()

    @pl.when(gives_cols & own_col)
    def _():
        out_cols[slot] = out_own[...]

    @pl.when(gives_cols & jnp.logical_not(own_col))
    def _():
        col_copy(0).start()

    @pl.when(gives_cols)
    def _():
        for d in range(1, NY):
            col_copy(d).start()

    for i in range(2):
        @pl.when(2 * v + i != dp)
        def _():
            copy(side_cols.at[i], side_cols.at[i], id_s.at[0, i], id_s.at[1, i], at(dc=1)).wait_recv()
            to_cols(i).wait_send()

    for e in range(2):
        @pl.when(jnp.logical_not(gives_rows & (c == e)))
        def _():
            copy(out_rows.at[e], out_rows.at[e], row_send.at[0], row_s.at[e], at(dc=1)).wait_recv()
        for i in range(2):
            @pl.when(jnp.logical_not((from_x == x) & (from_y(i) == y) & (c == e)))
            def _():
                n = 2 * i + e
                copy(out_cols.at[n], out_cols.at[n], col_send.at[0], col_s.at[n], at(dc=1)).wait_recv()

    high = lax.Precision.HIGHEST
    outs = lax.dot_general(
        out_rows[...].reshape(32, 128), out_cols[...].reshape(64, 128), NT, precision=high, preferred_element_type=F32
    )
    ins = lax.dot_general(
        side[3], side_cols[...].reshape(64, 128), NT, precision=high, preferred_element_type=F32
    )
    both = outs * ins
    sums = jnp.concatenate(
        [jnp.sum(both[16 * e : 16 * e + 16], axis=0, keepdims=True) for e in range(2)], axis=0
    )
    gram[...] = jnp.concatenate(
        [jnp.sum(sums[:, 16 * f : 16 * f + 16], axis=1, keepdims=True) for f in range(4)], axis=1
    )

    for made in pending:
        made.wait_send()

    @pl.when(gives_rows)
    def _():
        for n in range(7):
            row_copy(n).wait_send()

    @pl.when(gives_cols & jnp.logical_not(own_col))
    def _():
        col_copy(0).wait_send()

    @pl.when(gives_cols)
    def _():
        for d in range(1, NY):
            col_copy(d).wait_send()


def shards(hidden_states, positions, target_ids, head, out_factor, in_factor):
    voc_local, width = head.shape
    rank = out_factor.shape[1]

    def sems(*shape):
        return pltpu.SemaphoreType.DMA(shape)

    return pl.pallas_call(
        kernel,
        out_shape=jax.ShapeDtypeStruct((2, 4), F32),
        in_specs=[pl.BlockSpec(memory_space=pltpu.VMEM)] * 6,
        out_specs=pl.BlockSpec(memory_space=pltpu.VMEM),
        scratch_shapes=[
            pltpu.VMEM((2, NY, NL, 16, width), BF16),
            pltpu.VMEM((32, 128), BF16),
            pltpu.VMEM((384, rank), BF16),
            pltpu.VMEM((NY, voc_local, 128), F32),
            pltpu.VMEM((4, 3, 8, 128), F32),
            pltpu.VMEM((3, 7, 3, 8, 128), F32),
            pltpu.VMEM((2, NL, NY, 16, rank), F32),
            pltpu.VMEM((NL, NY, 16, rank), F32),
            pltpu.VMEM((NL, NY, 16, rank), F32),
            pltpu.VMEM((NX - 1, NY, 16, rank), F32),
            pltpu.VMEM((NY, 16, rank), F32),
            pltpu.VMEM((NY - 1, 16, rank), F32),
            pltpu.VMEM((16, rank), F32),
            pltpu.VMEM((NZ - 1, 16, rank), F32),
            pltpu.VMEM((4, 32, rank), F32),
            pltpu.VMEM((5, 32, rank), F32),
            pltpu.VMEM((2, 32, rank), F32),
            pltpu.VMEM((16, rank), F32),
            pltpu.VMEM((2, 16, rank), F32),
            pltpu.VMEM((4, 16, rank), F32),
            sems(2, 8), sems(2, 32), sems(2, 4), sems(2, 8), sems(2, 24), sems(2, 16), sems(2, 21),
            sems(2, 1), sems(2, 3), sems(2, 7), sems(2, 7), sems(2, 1), sems(2, 3), sems(2, 1), sems(2, 2),
            sems(2), sems(7), sems(4), sems(8),
        ],
        compiler_params=pltpu.CompilerParams(
            collective_id=0, has_side_effects=True, vmem_limit_bytes=48 * 1024 * 1024
        ),
        cost_estimate=pl.CostEstimate(flops=4 * 10**9, bytes_accessed=5 * 10**6, transcendentals=10**6),
    )(hidden_states, positions, target_ids, head, out_factor, in_factor)


def solution(mesh):
    placed = (
        P("dp", None),
        P("dp", None),
        P(),
        P(("dp", "vocab"), None),
        P(("dp", "vocab"), None),
        P("vocab", None),
    )
    return jax.shard_map(
        shards, mesh=mesh, in_specs=placed, out_specs=P("dp", "vocab"), check_vma=False
    )
```

```python
import jax
import jax.numpy as jnp
from jax import lax
from jax.experimental import pallas as pl
from jax.experimental.pallas import tpu as pltpu
from jax.sharding import PartitionSpec as P

entropy_weight = 0.2
MESH = pl.DeviceIdType.MESH
NX, NY, NZ, NL = 4, 8, 8, 4
FAR_FIRST = (4, 3, 5, 2, 6, 1, 7)
F32, BF16 = jnp.float32, jnp.bfloat16
NT = (((1,), (1,)), ((), ()))
TN = (((0,), (0,)), ((), ()))

QUARTER, S_DIRECT, T_DIRECT = 512, 1280, 1792
S_WIDE, WIDE = S_DIRECT + QUARTER, S_DIRECT + QUARTER + T_DIRECT
S_HALVES = ((0, S_WIDE // 256 * 128), (S_WIDE // 256 * 128, S_WIDE - S_WIDE // 256 * 128))
T_HALVES = ((0, T_DIRECT // 256 * 128), (T_DIRECT // 256 * 128, T_DIRECT - T_DIRECT // 256 * 128))


def device(x, y, z, c):
    return (lax.rem(z, NL) * NY + y, (z // NL) * 2 * NX + x * 2 + c)


def kernel(
    hidden_hbm, positions, targets, head_hbm, out_factor_hbm, in_factor_hbm, gram,
    hidden, head, out_factor, in_factor, by_example, sel, onehot, in_pad, logits, stats, packed, stats_in, by_rank, x_in, by_y, y_in, own, z_in,
    side, side_in, side_cols, out_own, out_rows, out_cols,
    s_y, o_y, s_z, t_z, t_y, x_s, sib_s, st_s, px_s, py_s, pz_s, is_s, ix_s, iz_s, id_s, row_s, row_send, col_s, col_send, load_s,
):
    dp, v = lax.axis_index("dp"), lax.axis_index("vocab")
    y, zl = lax.rem(dp, NY), dp // NY
    zh, x, c = v // (2 * NX), lax.rem(v, 2 * NX) // 2, lax.rem(v, 2)
    z = zh * NL + zl
    voc_local = head.shape[1]

    def at(dx=0, dy=0, dz=0, dc=0):
        return device(
            lax.rem(x + dx + NX, NX), lax.rem(y + dy + NY, NY), lax.rem(z + dz + NZ, NZ), lax.rem(c + dc, 2)
        )

    x_line = [(dx, dc) for dx in range(NX) for dc in range(2) if dx or dc]
    pending = []

    def copy(src, dst, sent, received, to):
        return pltpu.make_async_remote_copy(
            src_ref=src, dst_ref=dst, send_sem=sent, recv_sem=received, device_id=to, device_id_type=MESH
        )

    def send(src, dst, sems, index, to):
        made = copy(src, dst, sems.at[0, index], sems.at[1, index], to)
        made.start()
        pending.append(made)

    def settle():
        for made in pending:
            made.wait_send()
        pending.clear()

    def arrive(dst, sems, index):
        copy(dst, dst, sems.at[0, index], sems.at[1, index], at(dc=1)).wait_recv()

    loads = [
        pltpu.make_async_copy(src, dst, load_s.at[n])
        for n, (src, dst) in enumerate(
            ((hidden_hbm, hidden), (in_factor_hbm, in_factor), (head_hbm, head.at[c]), (out_factor_hbm, out_factor.at[c]))
        )
    ]
    for load in loads:
        load.start()

    gives_rows = zl == x
    gives_cols = zh == x // 2
    col_x, col_c = 2 * lax.rem(x, 2) + y // 4, lax.rem(y, 4) // 2
    from_x = zh * 2 + x // 2

    def from_y(i):
        return lax.rem(x, 2) * 4 + c * 2 + i

    own_col = jnp.logical_and(col_x == x, col_c == c)

    barrier = pltpu.get_barrier_semaphore()

    def greet(to):
        pl.semaphore_signal(barrier, inc=1, device_id=to, device_id_type=MESH)

    for dx, dc in x_line:
        greet(at(dx=dx, dc=dc))
    for d in range(1, NY):
        greet(at(dy=d))
        greet(at(dz=d))
    for i in range(2):
        @pl.when(2 * v + i != dp)
        def _():
            greet((2 * v + i, dp // 2))
        for e in range(2):
            @pl.when(jnp.logical_not((from_x == x) & (from_y(i) == y) & (c == e)))
            def _():
                greet(device(from_x, from_y(i), z, e))
    expected = 21 + 2 - (dp // 2 == v).astype(jnp.int32)
    expected += jnp.where(gives_cols, 8 - own_col.astype(jnp.int32), 0)

    place = jnp.concatenate(
        [positions[0:1, :], positions[1:2, :], jnp.full((1, 96), -1, jnp.int32)], axis=1
    )
    hot = (lax.broadcasted_iota(jnp.int32, (128, 128), 0) == place).astype(F32)
    onehot[...] = jnp.transpose(hot)[0:32].astype(BF16)
    mine = onehot[pl.ds(pl.multiple_of(c * 16, 16), 16), :]

    def quarter_of(d):
        return pl.multiple_of(S_DIRECT + T_DIRECT + QUARTER * lax.rem(x - d + NX, NX), 128)

    runs = [
        (0, S_DIRECT, 0),
        (S_DIRECT, QUARTER, quarter_of(0)),
        (S_WIDE, T_DIRECT, S_DIRECT),
        *[(WIDE + QUARTER * (d - 1), QUARTER, quarter_of(d)) for d in range(1, NX)],
    ]

    loads[0].wait()
    for start, size, whole in runs[:3]:
        sel[y, 0, :, start : start + size] = jnp.dot(
            mine, hidden[:, pl.ds(whole, size)], preferred_element_type=F32
        ).astype(BF16)

    pl.semaphore_wait(barrier, expected)

    def group(dy):
        return lax.rem(y + dy + NY, NY)

    def cols(start, size):
        return pl.ds(start, size)

    def s_piece(dy, dz, start=0, size=S_WIDE):
        return sel.at[group(dy), dz % NL, :, cols(start, size)]

    def t_piece(dz, start=0, size=T_DIRECT):
        return sel.at[y, dz % NL, :, cols(S_WIDE + start, size)]

    def t_block(dy, half):
        return sel.at[group(dy), pl.ds(1, NL - 1), :, cols(S_WIDE + T_HALVES[half][0], T_HALVES[half][1])]

    def y_index(dy):
        return dy - 1 if dy > 0 else 3 - dy

    def s_part(dy):
        return S_HALVES[0] if dy == -4 else S_HALVES[1] if dy == 4 else (0, S_WIDE)

    def s_forward(k):
        for dy, step in ((-k, 1), (k, -1)):
            piece = s_piece(dy, 0, *s_part(dy - step))
            send(piece, piece, s_y, y_index(dy - step), at(dy=step))

    def s_arrived(k):
        for dy in (-k, k):
            arrive(s_piece(dy, 0, *s_part(dy)), s_y, y_index(dy))

    def own_part(dy, part):
        start, size = T_HALVES[0] if part == -4 else T_HALVES[1] if part == 4 else (0, T_DIRECT)
        return sel.at[group(dy), 0, :, cols(S_WIDE + start, size)]

    def own_forward(k):
        for dy, step in ((-k, 1), (k, -1)):
            piece = own_part(dy, dy - step)
            send(piece, piece, o_y, y_index(dy - step), at(dy=step))

    def own_arrived(k):
        for dy in (-k, k):
            arrive(own_part(dy, dy), o_y, y_index(dy))

    def t_forward(k, half):
        for dy, step in ((-k, 1), (k, -1)):
            if k < 3 or half == (step < 0):
                send(t_block(dy, half), t_block(dy, half), t_y, 2 * y_index(dy - step) + half, at(dy=step))

    def t_arrived(k, half):
        for dy in (-k, k):
            if k < 4 or half == (dy > 0):
                arrive(t_block(dy, half), t_y, 2 * y_index(dy) + half)

    def z_moves(halves):
        whole = (0, halves[0][1] + halves[1][1])
        return ((1, *whole), (-1, *whole), (2, *halves[0]), (-2, *halves[1]))

    def s_z_sends(dy):
        for n, (dz, start, size) in enumerate(z_moves(S_HALVES)):
            send(s_piece(dy, 0, start, size), s_piece(dy, -dz, start, size), s_z, 4 * (dy % 8) + n, at(dz=dz))

    def s_z_arrive(dy):
        for n, (dz, start, size) in enumerate(z_moves(S_HALVES)):
            arrive(s_piece(dy, -dz, start, size), s_z, 4 * (dy % 8) + n)

    def pair(k):
        return (0,) if k == 0 else (4,) if k == 4 else (k, -k)

    def x_sends(dy):
        s_z_arrive(dy)
        for d in range(1, NX):
            send(
                sel.at[group(dy), :, :, cols(S_DIRECT, QUARTER)],
                sel.at[group(dy), :, :, cols(WIDE + QUARTER * (d - 1), QUARTER)],
                x_s, 3 * (dy % 8) + d - 1, at(dx=d),
            )

    def x_arrive(dy):
        for d in range(1, NX):
            arrive(sel.at[group(dy), :, :, cols(WIDE + QUARTER * (d - 1), QUARTER)], x_s, 3 * (dy % 8) + d - 1)

    def compute(*dys):
        total = [jnp.zeros((voc_local, 64 * len(dys)), F32) for _ in range(2)]
        for start, size, whole in runs:
            rows = [
                sel[group(dy), lax.rem(p - zl + NL, NL), :, start : start + size] for dy in dys for p in range(NL)
            ]
            rows = jnp.concatenate(rows, axis=0)
            for h in range(2):
                total[h] += lax.dot_general(head[h, :, pl.ds(whole, size)], rows, NT, preferred_element_type=F32)
        for n, dy in enumerate(dys):
            values = [total[h][:, 64 * n : 64 * n + 64] for h in range(2)]
            row = pl.ds(group(dy), 1)
            top = jnp.maximum(*[jnp.max(part, axis=0, keepdims=True) for part in values])
            power_sum, weighted = jnp.zeros_like(top), jnp.zeros_like(top)
            for h in range(2):
                lowered = values[h] - top
                power = jnp.exp(lowered)
                logits[group(dy), h] = values[h]
                power_sum += jnp.sum(power, axis=0, keepdims=True)
                weighted += jnp.sum(power * lowered, axis=0, keepdims=True)
            unused = jnp.ones((1, 64), F32)
            for n_stat, value in enumerate((top, power_sum, weighted)):
                stats[n_stat, row, :] = jnp.concatenate([value, unused], axis=1)

    def to_cols(i):
        there = lax.rem(dp, 2)
        return copy(side.at[3], side_cols.at[there], id_s.at[0, i], id_s.at[1, there], (2 * v + i, dp // 2))

    def t_relay(k, half):
        t_arrived(k, half)
        if k < 4:
            t_forward(k, half)

    s_forward(0)
    for n, (dz, start, size) in enumerate(z_moves(T_HALVES)):
        send(t_piece(0, start, size), t_piece(-dz, start, size), t_z, n, at(dz=dz))
    s_z_sends(0)

    loads[1].wait()
    window = pl.multiple_of(v * 320 - 64 * c, 128)
    in_pad[...] = jnp.zeros_like(in_pad)
    in_pad[pl.ds(pl.multiple_of(64 * c, 64), 320), :] = in_factor[...]
    chosen = jnp.dot(onehot[...], hidden[:, pl.ds(window, 384)], preferred_element_type=F32).astype(BF16)
    side[0] = jnp.dot(chosen, in_pad[...], preferred_element_type=F32)
    send(side.at[0], side_in.at[0], is_s, 0, at(dc=1))

    s_arrived(1)
    s_forward(1)
    own_forward(0)
    for n, (dz, start, size) in enumerate(z_moves(T_HALVES)):
        arrive(t_piece(-dz, start, size), t_z, n)
    t_forward(0, 0)
    s_z_sends(1)
    t_forward(0, 1)
    by_example[...] = jnp.transpose(
        jnp.pad(targets[...], ((0, 112), (0, 64))).astype(F32)
    )[0:64].astype(jnp.int32)
    for load in loads[2:]:
        load.wait()
    send(head.at[c], head.at[c], sib_s, 0, at(dc=1))
    send(out_factor.at[c], out_factor.at[c], sib_s, 1, at(dc=1))
    s_arrived(2)
    s_forward(2)
    own_arrived(1)
    own_forward(1)
    x_sends(0)
    s_z_sends(-1)
    arrive(side_in.at[0], is_s, 0)
    side[1] = side[0] + side_in[0]
    for d in range(1, NX):
        send(side.at[1], side_in.at[d], ix_s, d - 1, at(dx=d))
    t_relay(1, 0)
    s_arrived(3)
    s_forward(3)
    own_arrived(2)
    own_forward(2)
    s_z_sends(2)
    x_sends(1)
    t_relay(1, 1)
    s_arrived(4)
    own_arrived(3)
    own_forward(3)
    s_z_sends(-2)
    x_sends(-1)
    x_arrive(0)
    for d in range(1, NX):
        arrive(side_in.at[d], ix_s, d - 1)
    side[2] = side[1] + side_in[1] + side_in[2] + side_in[3]
    send(side.at[2], side_in.at[4], iz_s, 0, at(dz=4))
    t_relay(2, 0)
    s_z_sends(3)
    x_sends(2)
    x_arrive(1)
    t_relay(2, 1)
    arrive(head.at[1 - c], sib_s, 0)
    arrive(out_factor.at[1 - c], sib_s, 1)
    compute(0, 1)
    s_z_sends(-3)
    x_sends(-2)
    x_arrive(-1)
    arrive(side_in.at[4], iz_s, 0)
    side[3] = side[2] + side_in[4]
    for i in range(2):
        @pl.when(2 * v + i == dp)
        def _():
            side_cols[i] = side[3]

        @pl.when(2 * v + i != dp)
        def _():
            to_cols(i).start()
    t_relay(3, 0)
    s_z_sends(4)
    x_sends(3)
    x_arrive(2)
    t_relay(3, 1)
    x_sends(-3)
    x_arrive(-2)
    own_arrived(4)
    t_relay(4, 0)
    t_relay(4, 1)
    x_sends(4)
    compute(-1, 2)
    x_arrive(3)
    compute(-2, 3)
    x_arrive(-3)
    x_arrive(4)
    compute(-3, 4)

    def pack(*values):
        return jnp.concatenate([*values, jnp.zeros((4, 128), F32)], axis=0)

    packed[0] = pack(
        *[jnp.concatenate([stats[n, 0:4, 0:64], stats[n, 4:8, 0:64]], axis=1) for n in range(3)]
    )

    def merge(stage, peers):
        for n, to in enumerate(peers):
            send(packed.at[stage], stats_in.at[stage, n], st_s, 7 * stage + n, to)
        if stage:
            settle()
        for n in range(len(peers)):
            arrive(stats_in.at[stage, n], st_s, 7 * stage + n)
        parts = [packed[stage]] + [stats_in[stage, n] for n in range(len(peers))]
        top = parts[0][0:4]
        for part in parts[1:]:
            top = jnp.maximum(top, part[0:4])
        total, weighted = jnp.zeros_like(top), jnp.zeros_like(top)
        for part in parts:
            lower = part[0:4] - top
            scale = jnp.exp(lower)
            total += scale * part[4:8]
            weighted += scale * (part[8:12] + lower * part[4:8])
        packed[stage + 1] = pack(top, total, weighted)

    merge(0, [at(dx=d) for d in (2, 1, 3)])
    merge(1, [at(dy=d) for d in FAR_FIRST])
    merge(2, [at(dz=d) for d in FAR_FIRST])
    log_sum = jnp.log(packed[3, 4:8, :])
    log_totals = packed[3, 0:4, :] + log_sum
    entropies = log_sum - packed[3, 8:12, :] / packed[3, 4:8, :]

    wanted = jnp.concatenate(
        [
            jnp.where(c == 0, *[by_example[pl.ds(16 * b + e, 8, stride=2), 0:16] for e in range(2)])
            for b in range(NL)
        ],
        axis=1,
    )
    ids = lax.broadcasted_iota(jnp.int32, (voc_local, 64), 0) + (dp * 2 * NX * 2 + v - c) * voc_local
    for g in range(NY):
        spot = (slice(g % 4, g % 4 + 1), slice(g // 4 * 64, g // 4 * 64 + 64))
        log_total, entropy = log_totals[spot], entropies[spot]
        result = jnp.zeros((64, out_factor.shape[2]), F32)
        for h in range(2):
            lowered = logits[g, h] - log_total
            probs = jnp.exp(lowered)
            hits = (ids + h * voc_local == wanted[g : g + 1, :]).astype(F32)
            grads = probs - hits + entropy_weight * probs * (lowered + entropy)
            result += lax.dot_general(grads.astype(BF16), out_factor[h], TN, preferred_element_type=F32)
        by_rank[:, g] = result.astype(BF16).reshape(NL, 16, 128)

    for d in (2, 1, 3):
        send(by_rank.at[lax.rem(x + d, NX)], x_in.at[d - 1], px_s, d - 1, at(dx=d))
    for d in range(1, NX):
        arrive(x_in.at[d - 1], px_s, d - 1)
    by_y[...] = by_rank[x].astype(F32) + x_in[0].astype(F32) + x_in[1].astype(F32) + x_in[2].astype(F32)
    for d in FAR_FIRST:
        send(by_y.at[lax.rem(y + d, NY)], y_in.at[d - 1], py_s, d - 1, at(dy=d))
    for d in range(1, NY):
        arrive(y_in.at[d - 1], py_s, d - 1)
    own[...] = by_y[y] + jnp.sum(y_in[...], axis=0)
    for d in FAR_FIRST:
        send(own, z_in.at[d - 1], pz_s, d - 1, at(dz=d))
    settle()
    for d in range(1, NZ):
        arrive(z_in.at[d - 1], pz_s, d - 1)
    out_own[...] = own[...] + jnp.sum(z_in[...], axis=0)

    def row_copy(n):
        dx, dc = x_line[n]
        return copy(out_own, out_rows.at[c], row_send.at[n], row_s.at[c], at(dx=dx, dc=dc))

    slot = lax.rem(y, 2) * 2 + c

    def col_copy(d):
        to = device(col_x, lax.rem(y + d, NY), z, col_c)
        return copy(out_own, out_cols.at[slot], col_send.at[d], col_s.at[slot], to)

    @pl.when(gives_cols & own_col)
    def _():
        out_cols[slot] = out_own[...]

    @pl.when(gives_cols & jnp.logical_not(own_col))
    def _():
        col_copy(0).start()

    @pl.when(gives_cols)
    def _():
        for d in FAR_FIRST:
            col_copy(d).start()

    @pl.when(gives_rows)
    def _():
        out_rows[c] = out_own[...]
        for n in range(7):
            row_copy(n).start()

    for i in range(2):
        @pl.when(2 * v + i != dp)
        def _():
            copy(side_cols.at[i], side_cols.at[i], id_s.at[0, i], id_s.at[1, i], at(dc=1)).wait_recv()
            to_cols(i).wait_send()

    settle()
    ins = lax.dot_general(
        side[3], side_cols[...].reshape(64, 128), NT, precision=lax.Precision.HIGHEST, preferred_element_type=F32
    )
    for e in range(2):
        @pl.when(jnp.logical_not(gives_rows & (c == e)))
        def _():
            copy(out_rows.at[e], out_rows.at[e], row_send.at[0], row_s.at[e], at(dc=1)).wait_recv()
        for i in range(2):
            @pl.when(jnp.logical_not((from_x == x) & (from_y(i) == y) & (c == e)))
            def _():
                n = 2 * i + e
                copy(out_cols.at[n], out_cols.at[n], col_send.at[0], col_s.at[n], at(dc=1)).wait_recv()

    high = lax.Precision.HIGHEST
    outs = lax.dot_general(
        out_rows[...].reshape(32, 128), out_cols[...].reshape(64, 128), NT, precision=high, preferred_element_type=F32
    )
    both = outs * ins
    sums = jnp.concatenate(
        [jnp.sum(both[16 * e : 16 * e + 16], axis=0, keepdims=True) for e in range(2)], axis=0
    )
    gram[...] = jnp.concatenate(
        [jnp.sum(sums[:, 16 * f : 16 * f + 16], axis=1, keepdims=True) for f in range(4)], axis=1
    )

    @pl.when(gives_rows)
    def _():
        for n in range(7):
            row_copy(n).wait_send()

    @pl.when(gives_cols & jnp.logical_not(own_col))
    def _():
        col_copy(0).wait_send()

    @pl.when(gives_cols)
    def _():
        for d in range(1, NY):
            col_copy(d).wait_send()


def shards(hidden_states, positions, target_ids, head, out_factor, in_factor):
    voc_local, width = head.shape
    rank = out_factor.shape[1]

    def sems(*shape):
        return pltpu.SemaphoreType.DMA(shape)

    return pl.pallas_call(
        kernel,
        out_shape=jax.ShapeDtypeStruct((2, 4), F32),
        in_specs=[
            pl.BlockSpec(memory_space=space)
            for space in (pltpu.HBM, pltpu.VMEM, pltpu.VMEM, pltpu.HBM, pltpu.HBM, pltpu.HBM)
        ],
        out_specs=pl.BlockSpec(memory_space=pltpu.VMEM),
        scratch_shapes=[
            pltpu.VMEM(hidden_states.shape, BF16),
            pltpu.VMEM((2, *head.shape), BF16),
            pltpu.VMEM((2, *out_factor.shape), BF16),
            pltpu.VMEM(in_factor.shape, BF16),
            pltpu.VMEM((64, 128), jnp.int32),
            pltpu.VMEM((NY, NL, 16, width), BF16),
            pltpu.VMEM((32, 128), BF16),
            pltpu.VMEM((384, rank), BF16),
            pltpu.VMEM((NY, 2, voc_local, 64), F32),
            pltpu.VMEM((3, 8, 128), F32),
            pltpu.VMEM((4, 16, 128), F32),
            pltpu.VMEM((3, 7, 16, 128), F32),
            pltpu.VMEM((NL, NY, 16, rank), BF16),
            pltpu.VMEM((NX - 1, NY, 16, rank), BF16),
            pltpu.VMEM((NY, 16, rank), F32),
            pltpu.VMEM((NY - 1, 16, rank), F32),
            pltpu.VMEM((16, rank), F32),
            pltpu.VMEM((NZ - 1, 16, rank), F32),
            pltpu.VMEM((4, 32, rank), F32),
            pltpu.VMEM((5, 32, rank), F32),
            pltpu.VMEM((2, 32, rank), F32),
            pltpu.VMEM((16, rank), F32),
            pltpu.VMEM((2, 16, rank), F32),
            pltpu.VMEM((4, 16, rank), F32),
            sems(2, 8), sems(2, 8), sems(2, 32), sems(2, 4), sems(2, 16), sems(2, 24), sems(2, 2), sems(2, 21),
            sems(2, 3), sems(2, 7), sems(2, 7), sems(2, 1), sems(2, 3), sems(2, 1), sems(2, 2),
            sems(2), sems(7), sems(4), sems(8), sems(4),
        ],
        compiler_params=pltpu.CompilerParams(
            collective_id=0, has_side_effects=True, vmem_limit_bytes=60 * 1024 * 1024
        ),
        cost_estimate=pl.CostEstimate(flops=4 * 10**9, bytes_accessed=5 * 10**6, transcendentals=10**6),
    )(hidden_states, positions, target_ids.T, head, out_factor, in_factor)


def solution(mesh):
    placed = (
        P("dp", None),
        P("dp", None),
        P(),
        P(("dp", "vocab"), None),
        P(("dp", "vocab"), None),
        P("vocab", None),
    )
    return jax.shard_map(
        shards, mesh=mesh, in_specs=placed, out_specs=P("dp", "vocab"), check_vma=False
    )
```

```python
import jax
import jax.numpy as jnp
from jax import lax
from jax.experimental import pallas as pl
from jax.experimental.pallas import tpu as pltpu
from jax.sharding import PartitionSpec as P

entropy_weight = 0.2
MESH = pl.DeviceIdType.MESH
NX, NY, NZ, NL = 4, 8, 8, 4
FAR_FIRST = (4, 3, 5, 2, 6, 1, 7)
F32, BF16 = jnp.float32, jnp.bfloat16
NT = (((1,), (1,)), ((), ()))
TN = (((0,), (0,)), ((), ()))

QUARTER, S_DIRECT, T_DIRECT = 512, 1024, 2048
S_WIDE, WIDE = S_DIRECT + QUARTER, S_DIRECT + QUARTER + T_DIRECT
S_HALVES = ((0, S_WIDE // 256 * 128), (S_WIDE // 256 * 128, S_WIDE - S_WIDE // 256 * 128))
T_HALVES = ((0, T_DIRECT // 256 * 128), (T_DIRECT // 256 * 128, T_DIRECT - T_DIRECT // 256 * 128))


def device(x, y, z, c):
    return (lax.rem(z, NL) * NY + y, (z // NL) * 2 * NX + x * 2 + c)


def kernel(
    hidden_hbm, positions, targets, head_hbm, out_factor_hbm, in_factor_hbm, gram,
    hidden, head, out_factor, in_factor, by_example, sel, onehot, in_pad, logits, stats, packed, stats_in, by_rank, x_in, by_y, y_in, own, z_in,
    side, side_in, side_cols, out_own, out_rows, out_cols,
    s_y, o_y, s_z, t_z, t_y, x_s, sib_s, st_s, px_s, py_s, pz_s, is_s, ix_s, iz_s, id_s, row_s, row_send, col_s, col_send, load_s,
):
    dp, v = lax.axis_index("dp"), lax.axis_index("vocab")
    y, zl = lax.rem(dp, NY), dp // NY
    zh, x, c = v // (2 * NX), lax.rem(v, 2 * NX) // 2, lax.rem(v, 2)
    z = zh * NL + zl
    voc_local = head.shape[1]

    def at(dx=0, dy=0, dz=0, dc=0):
        return device(
            lax.rem(x + dx + NX, NX), lax.rem(y + dy + NY, NY), lax.rem(z + dz + NZ, NZ), lax.rem(c + dc, 2)
        )

    x_line = [(dx, dc) for dx in range(NX) for dc in range(2) if dx or dc]
    pending = []

    def copy(src, dst, sent, received, to):
        return pltpu.make_async_remote_copy(
            src_ref=src, dst_ref=dst, send_sem=sent, recv_sem=received, device_id=to, device_id_type=MESH
        )

    def send(src, dst, sems, index, to):
        made = copy(src, dst, sems.at[0, index], sems.at[1, index], to)
        made.start()
        pending.append(made)

    def settle():
        for made in pending:
            made.wait_send()
        pending.clear()

    def arrive(dst, sems, index):
        copy(dst, dst, sems.at[0, index], sems.at[1, index], at(dc=1)).wait_recv()

    loads = [
        pltpu.make_async_copy(src, dst, load_s.at[n])
        for n, (src, dst) in enumerate(
            ((hidden_hbm, hidden), (in_factor_hbm, in_factor), (head_hbm, head.at[c]), (out_factor_hbm, out_factor.at[c]))
        )
    ]
    for load in loads:
        load.start()

    gives_rows = zl == x
    gives_cols = zh == x // 2
    col_x, col_c = 2 * lax.rem(x, 2) + y // 4, lax.rem(y, 4) // 2
    from_x = zh * 2 + x // 2

    def from_y(i):
        return lax.rem(x, 2) * 4 + c * 2 + i

    own_col = jnp.logical_and(col_x == x, col_c == c)

    barrier = pltpu.get_barrier_semaphore()

    def greet(to):
        pl.semaphore_signal(barrier, inc=1, device_id=to, device_id_type=MESH)

    for dx, dc in x_line:
        greet(at(dx=dx, dc=dc))
    for d in range(1, NY):
        greet(at(dy=d))
        greet(at(dz=d))
    for i in range(2):
        @pl.when(2 * v + i != dp)
        def _():
            greet((2 * v + i, dp // 2))
        for e in range(2):
            @pl.when(jnp.logical_not((from_x == x) & (from_y(i) == y) & (c == e)))
            def _():
                greet(device(from_x, from_y(i), z, e))
    expected = 21 + 2 - (dp // 2 == v).astype(jnp.int32)
    expected += jnp.where(gives_cols, 8 - own_col.astype(jnp.int32), 0)

    place = jnp.concatenate(
        [positions[0:1, :], positions[1:2, :], jnp.full((1, 96), -1, jnp.int32)], axis=1
    )
    hot = (lax.broadcasted_iota(jnp.int32, (128, 128), 0) == place).astype(F32)
    onehot[...] = jnp.transpose(hot)[0:32].astype(BF16)
    mine = onehot[pl.ds(pl.multiple_of(c * 16, 16), 16), :]

    def quarter_of(d):
        return pl.multiple_of(S_DIRECT + T_DIRECT + QUARTER * lax.rem(x - d + NX, NX), 128)

    runs = [
        (0, S_DIRECT, 0),
        (S_DIRECT, QUARTER, quarter_of(0)),
        (S_WIDE, T_DIRECT, S_DIRECT),
        *[(WIDE + QUARTER * (d - 1), QUARTER, quarter_of(d)) for d in range(1, NX)],
    ]

    loads[0].wait()
    for start, size, whole in runs[:3]:
        sel[y, 0, :, start : start + size] = jnp.dot(
            mine, hidden[:, pl.ds(whole, size)], preferred_element_type=F32
        ).astype(BF16)

    pl.semaphore_wait(barrier, expected)

    def group(dy):
        return lax.rem(y + dy + NY, NY)

    def cols(start, size):
        return pl.ds(start, size)

    def s_piece(dy, dz, start=0, size=S_WIDE):
        return sel.at[group(dy), dz % NL, :, cols(start, size)]

    def t_piece(dz, start=0, size=T_DIRECT):
        return sel.at[y, dz % NL, :, cols(S_WIDE + start, size)]

    def t_block(dy, half):
        return sel.at[group(dy), pl.ds(1, NL - 1), :, cols(S_WIDE + T_HALVES[half][0], T_HALVES[half][1])]

    def y_index(dy):
        return dy - 1 if dy > 0 else 3 - dy

    def s_part(dy):
        return S_HALVES[0] if dy == -4 else S_HALVES[1] if dy == 4 else (0, S_WIDE)

    def s_forward(k):
        for dy, step in ((-k, 1), (k, -1)):
            piece = s_piece(dy, 0, *s_part(dy - step))
            send(piece, piece, s_y, y_index(dy - step), at(dy=step))

    def s_arrived(k):
        for dy in (-k, k):
            arrive(s_piece(dy, 0, *s_part(dy)), s_y, y_index(dy))

    def own_part(dy, part):
        start, size = T_HALVES[0] if part == -4 else T_HALVES[1] if part == 4 else (0, T_DIRECT)
        return sel.at[group(dy), 0, :, cols(S_WIDE + start, size)]

    def own_forward(k):
        for dy, step in ((-k, 1), (k, -1)):
            piece = own_part(dy, dy - step)
            send(piece, piece, o_y, y_index(dy - step), at(dy=step))

    def own_arrived(k):
        for dy in (-k, k):
            arrive(own_part(dy, dy), o_y, y_index(dy))

    def t_forward(k, half):
        for dy, step in ((-k, 1), (k, -1)):
            if k < 3 or half == (step < 0):
                send(t_block(dy, half), t_block(dy, half), t_y, 2 * y_index(dy - step) + half, at(dy=step))

    def t_arrived(k, half):
        for dy in (-k, k):
            if k < 4 or half == (dy > 0):
                arrive(t_block(dy, half), t_y, 2 * y_index(dy) + half)

    def z_moves(halves):
        whole = (0, halves[0][1] + halves[1][1])
        return ((1, *whole), (-1, *whole), (2, *halves[0]), (-2, *halves[1]))

    def s_z_sends(dy):
        for n, (dz, start, size) in enumerate(z_moves(S_HALVES)):
            send(s_piece(dy, 0, start, size), s_piece(dy, -dz, start, size), s_z, 4 * (dy % 8) + n, at(dz=dz))

    def s_z_arrive(dy):
        for n, (dz, start, size) in enumerate(z_moves(S_HALVES)):
            arrive(s_piece(dy, -dz, start, size), s_z, 4 * (dy % 8) + n)

    def pair(k):
        return (0,) if k == 0 else (4,) if k == 4 else (k, -k)

    def x_sends(dy):
        s_z_arrive(dy)
        for d in range(1, NX):
            send(
                sel.at[group(dy), :, :, cols(S_DIRECT, QUARTER)],
                sel.at[group(dy), :, :, cols(WIDE + QUARTER * (d - 1), QUARTER)],
                x_s, 3 * (dy % 8) + d - 1, at(dx=d),
            )

    def x_arrive(dy):
        for d in range(1, NX):
            arrive(sel.at[group(dy), :, :, cols(WIDE + QUARTER * (d - 1), QUARTER)], x_s, 3 * (dy % 8) + d - 1)

    def compute(*dys):
        total = [jnp.zeros((voc_local, 64 * len(dys)), F32) for _ in range(2)]
        for start, size, whole in runs:
            rows = [
                sel[group(dy), lax.rem(p - zl + NL, NL), :, start : start + size] for dy in dys for p in range(NL)
            ]
            rows = jnp.concatenate(rows, axis=0)
            for h in range(2):
                total[h] += lax.dot_general(head[h, :, pl.ds(whole, size)], rows, NT, preferred_element_type=F32)
        for n, dy in enumerate(dys):
            values = [total[h][:, 64 * n : 64 * n + 64] for h in range(2)]
            row = pl.ds(group(dy), 1)
            top = jnp.maximum(*[jnp.max(part, axis=0, keepdims=True) for part in values])
            power_sum, weighted = jnp.zeros_like(top), jnp.zeros_like(top)
            for h in range(2):
                lowered = values[h] - top
                power = jnp.exp(lowered)
                logits[group(dy), h] = values[h]
                power_sum += jnp.sum(power, axis=0, keepdims=True)
                weighted += jnp.sum(power * lowered, axis=0, keepdims=True)
            unused = jnp.ones((1, 64), F32)
            for n_stat, value in enumerate((top, power_sum, weighted)):
                stats[n_stat, row, :] = jnp.concatenate([value, unused], axis=1)

    def to_cols(i):
        there = lax.rem(dp, 2)
        return copy(side.at[3], side_cols.at[there], id_s.at[0, i], id_s.at[1, there], (2 * v + i, dp // 2))

    def t_relay(k, half):
        t_arrived(k, half)
        if k < 4:
            t_forward(k, half)

    s_forward(0)
    for n, (dz, start, size) in enumerate(z_moves(T_HALVES)):
        send(t_piece(0, start, size), t_piece(-dz, start, size), t_z, n, at(dz=dz))
    s_z_sends(0)

    loads[1].wait()
    window = pl.multiple_of(v * 320 - 64 * c, 128)
    in_pad[...] = jnp.zeros_like(in_pad)
    in_pad[pl.ds(pl.multiple_of(64 * c, 64), 320), :] = in_factor[...]
    chosen = jnp.dot(onehot[...], hidden[:, pl.ds(window, 384)], preferred_element_type=F32).astype(BF16)
    side[0] = jnp.dot(chosen, in_pad[...], preferred_element_type=F32)
    send(side.at[0], side_in.at[0], is_s, 0, at(dc=1))

    s_arrived(1)
    s_forward(1)
    own_forward(0)
    for n, (dz, start, size) in enumerate(z_moves(T_HALVES)):
        arrive(t_piece(-dz, start, size), t_z, n)
    t_forward(0, 0)
    s_z_sends(1)
    t_forward(0, 1)
    by_example[...] = jnp.transpose(
        jnp.pad(targets[...], ((0, 112), (0, 64))).astype(F32)
    )[0:64].astype(jnp.int32)
    for load in loads[2:]:
        load.wait()
    send(head.at[c], head.at[c], sib_s, 0, at(dc=1))
    send(out_factor.at[c], out_factor.at[c], sib_s, 1, at(dc=1))
    s_arrived(2)
    s_forward(2)
    own_arrived(1)
    own_forward(1)
    x_sends(0)
    s_z_sends(-1)
    arrive(side_in.at[0], is_s, 0)
    side[1] = side[0] + side_in[0]
    for d in range(1, NX):
        send(side.at[1], side_in.at[d], ix_s, d - 1, at(dx=d))
    t_relay(1, 0)
    s_arrived(3)
    s_forward(3)
    own_arrived(2)
    own_forward(2)
    s_z_sends(2)
    x_sends(1)
    t_relay(1, 1)
    s_arrived(4)
    own_arrived(3)
    own_forward(3)
    s_z_sends(-2)
    x_sends(-1)
    x_arrive(0)
    for d in range(1, NX):
        arrive(side_in.at[d], ix_s, d - 1)
    side[2] = side[1] + side_in[1] + side_in[2] + side_in[3]
    send(side.at[2], side_in.at[4], iz_s, 0, at(dz=4))
    t_relay(2, 0)
    s_z_sends(3)
    x_sends(2)
    x_arrive(1)
    t_relay(2, 1)
    arrive(head.at[1 - c], sib_s, 0)
    arrive(out_factor.at[1 - c], sib_s, 1)
    compute(0, 1)
    s_z_sends(-3)
    x_sends(-2)
    x_arrive(-1)
    arrive(side_in.at[4], iz_s, 0)
    side[3] = side[2] + side_in[4]
    for i in range(2):
        @pl.when(2 * v + i == dp)
        def _():
            side_cols[i] = side[3]

        @pl.when(2 * v + i != dp)
        def _():
            to_cols(i).start()
    t_relay(3, 0)
    s_z_sends(4)
    x_sends(3)
    x_arrive(2)
    t_relay(3, 1)
    x_sends(-3)
    x_arrive(-2)
    own_arrived(4)
    t_relay(4, 0)
    t_relay(4, 1)
    x_sends(4)
    compute(-1, 2)
    x_arrive(3)
    compute(-2, 3)
    x_arrive(-3)
    x_arrive(4)
    compute(-3, 4)

    def pack(*values):
        return jnp.concatenate([*values, jnp.zeros((4, 128), F32)], axis=0)

    packed[0] = pack(
        *[jnp.concatenate([stats[n, 0:4, 0:64], stats[n, 4:8, 0:64]], axis=1) for n in range(3)]
    )

    def merge(stage, peers):
        for n, to in enumerate(peers):
            send(packed.at[stage], stats_in.at[stage, n], st_s, 7 * stage + n, to)
        if stage:
            settle()
        for n in range(len(peers)):
            arrive(stats_in.at[stage, n], st_s, 7 * stage + n)
        parts = [packed[stage]] + [stats_in[stage, n] for n in range(len(peers))]
        top = parts[0][0:4]
        for part in parts[1:]:
            top = jnp.maximum(top, part[0:4])
        total, weighted = jnp.zeros_like(top), jnp.zeros_like(top)
        for part in parts:
            lower = part[0:4] - top
            scale = jnp.exp(lower)
            total += scale * part[4:8]
            weighted += scale * (part[8:12] + lower * part[4:8])
        packed[stage + 1] = pack(top, total, weighted)

    merge(0, [at(dx=d) for d in (2, 1, 3)])
    merge(1, [at(dy=d) for d in FAR_FIRST])
    merge(2, [at(dz=d) for d in FAR_FIRST])
    log_sum = jnp.log(packed[3, 4:8, :])
    log_totals = packed[3, 0:4, :] + log_sum
    entropies = log_sum - packed[3, 8:12, :] / packed[3, 4:8, :]

    wanted = jnp.concatenate(
        [
            jnp.where(c == 0, *[by_example[pl.ds(16 * b + e, 8, stride=2), 0:16] for e in range(2)])
            for b in range(NL)
        ],
        axis=1,
    )
    ids = lax.broadcasted_iota(jnp.int32, (voc_local, 64), 0) + (dp * 2 * NX * 2 + v - c) * voc_local
    for g in range(NY):
        spot = (slice(g % 4, g % 4 + 1), slice(g // 4 * 64, g // 4 * 64 + 64))
        log_total, entropy = log_totals[spot], entropies[spot]
        result = jnp.zeros((64, out_factor.shape[2]), F32)
        for h in range(2):
            lowered = logits[g, h] - log_total
            probs = jnp.exp(lowered)
            hits = (ids + h * voc_local == wanted[g : g + 1, :]).astype(F32)
            grads = probs - hits + entropy_weight * probs * (lowered + entropy)
            result += lax.dot_general(grads.astype(BF16), out_factor[h], TN, preferred_element_type=F32)
        by_rank[:, g] = result.astype(BF16).reshape(NL, 16, 128)

    for d in (2, 1, 3):
        send(by_rank.at[lax.rem(x + d, NX)], x_in.at[d - 1], px_s, d - 1, at(dx=d))
    for d in range(1, NX):
        arrive(x_in.at[d - 1], px_s, d - 1)
    by_y[...] = by_rank[x].astype(F32) + x_in[0].astype(F32) + x_in[1].astype(F32) + x_in[2].astype(F32)
    for d in FAR_FIRST:
        send(by_y.at[lax.rem(y + d, NY)], y_in.at[d - 1], py_s, d - 1, at(dy=d))
    for d in range(1, NY):
        arrive(y_in.at[d - 1], py_s, d - 1)
    own[...] = by_y[y] + jnp.sum(y_in[...], axis=0)
    for d in FAR_FIRST:
        send(own, z_in.at[d - 1], pz_s, d - 1, at(dz=d))
    settle()
    for d in range(1, NZ):
        arrive(z_in.at[d - 1], pz_s, d - 1)
    out_own[...] = own[...] + jnp.sum(z_in[...], axis=0)

    def row_copy(n):
        dx, dc = x_line[n]
        return copy(out_own, out_rows.at[c], row_send.at[n], row_s.at[c], at(dx=dx, dc=dc))

    slot = lax.rem(y, 2) * 2 + c

    def col_copy(d):
        to = device(col_x, lax.rem(y + d, NY), z, col_c)
        return copy(out_own, out_cols.at[slot], col_send.at[d], col_s.at[slot], to)

    @pl.when(gives_cols & own_col)
    def _():
        out_cols[slot] = out_own[...]

    @pl.when(gives_cols & jnp.logical_not(own_col))
    def _():
        col_copy(0).start()

    @pl.when(gives_cols)
    def _():
        for d in FAR_FIRST:
            col_copy(d).start()

    @pl.when(gives_rows)
    def _():
        out_rows[c] = out_own[...]
        for n in range(7):
            row_copy(n).start()

    for i in range(2):
        @pl.when(2 * v + i != dp)
        def _():
            copy(side_cols.at[i], side_cols.at[i], id_s.at[0, i], id_s.at[1, i], at(dc=1)).wait_recv()
            to_cols(i).wait_send()

    settle()
    ins = lax.dot_general(
        side[3], side_cols[...].reshape(64, 128), NT, precision=lax.Precision.HIGHEST, preferred_element_type=F32
    )
    for e in range(2):
        @pl.when(jnp.logical_not(gives_rows & (c == e)))
        def _():
            copy(out_rows.at[e], out_rows.at[e], row_send.at[0], row_s.at[e], at(dc=1)).wait_recv()
        for i in range(2):
            @pl.when(jnp.logical_not((from_x == x) & (from_y(i) == y) & (c == e)))
            def _():
                n = 2 * i + e
                copy(out_cols.at[n], out_cols.at[n], col_send.at[0], col_s.at[n], at(dc=1)).wait_recv()

    high = lax.Precision.HIGHEST
    outs = lax.dot_general(
        out_rows[...].reshape(32, 128), out_cols[...].reshape(64, 128), NT, precision=high, preferred_element_type=F32
    )
    both = outs * ins
    sums = jnp.concatenate(
        [jnp.sum(both[16 * e : 16 * e + 16], axis=0, keepdims=True) for e in range(2)], axis=0
    )
    gram[...] = jnp.concatenate(
        [jnp.sum(sums[:, 16 * f : 16 * f + 16], axis=1, keepdims=True) for f in range(4)], axis=1
    )

    @pl.when(gives_rows)
    def _():
        for n in range(7):
            row_copy(n).wait_send()

    @pl.when(gives_cols & jnp.logical_not(own_col))
    def _():
        col_copy(0).wait_send()

    @pl.when(gives_cols)
    def _():
        for d in range(1, NY):
            col_copy(d).wait_send()


def shards(hidden_states, positions, target_ids, head, out_factor, in_factor):
    voc_local, width = head.shape
    rank = out_factor.shape[1]

    def sems(*shape):
        return pltpu.SemaphoreType.DMA(shape)

    return pl.pallas_call(
        kernel,
        out_shape=jax.ShapeDtypeStruct((2, 4), F32),
        in_specs=[
            pl.BlockSpec(memory_space=space)
            for space in (pltpu.HBM, pltpu.VMEM, pltpu.VMEM, pltpu.HBM, pltpu.HBM, pltpu.HBM)
        ],
        out_specs=pl.BlockSpec(memory_space=pltpu.VMEM),
        scratch_shapes=[
            pltpu.VMEM(hidden_states.shape, BF16),
            pltpu.VMEM((2, *head.shape), BF16),
            pltpu.VMEM((2, *out_factor.shape), BF16),
            pltpu.VMEM(in_factor.shape, BF16),
            pltpu.VMEM((64, 128), jnp.int32),
            pltpu.VMEM((NY, NL, 16, width), BF16),
            pltpu.VMEM((32, 128), BF16),
            pltpu.VMEM((384, rank), BF16),
            pltpu.VMEM((NY, 2, voc_local, 64), F32),
            pltpu.VMEM((3, 8, 128), F32),
            pltpu.VMEM((4, 16, 128), F32),
            pltpu.VMEM((3, 7, 16, 128), F32),
            pltpu.VMEM((NL, NY, 16, rank), BF16),
            pltpu.VMEM((NX - 1, NY, 16, rank), BF16),
            pltpu.VMEM((NY, 16, rank), F32),
            pltpu.VMEM((NY - 1, 16, rank), F32),
            pltpu.VMEM((16, rank), F32),
            pltpu.VMEM((NZ - 1, 16, rank), F32),
            pltpu.VMEM((4, 32, rank), F32),
            pltpu.VMEM((5, 32, rank), F32),
            pltpu.VMEM((2, 32, rank), F32),
            pltpu.VMEM((16, rank), F32),
            pltpu.VMEM((2, 16, rank), F32),
            pltpu.VMEM((4, 16, rank), F32),
            sems(2, 8), sems(2, 8), sems(2, 32), sems(2, 4), sems(2, 16), sems(2, 24), sems(2, 2), sems(2, 21),
            sems(2, 3), sems(2, 7), sems(2, 7), sems(2, 1), sems(2, 3), sems(2, 1), sems(2, 2),
            sems(2), sems(7), sems(4), sems(8), sems(4),
        ],
        compiler_params=pltpu.CompilerParams(
            collective_id=0, has_side_effects=True, vmem_limit_bytes=60 * 1024 * 1024
        ),
        cost_estimate=pl.CostEstimate(flops=4 * 10**9, bytes_accessed=5 * 10**6, transcendentals=10**6),
    )(hidden_states, positions, target_ids.T, head, out_factor, in_factor)


def solution(mesh):
    placed = (
        P("dp", None),
        P("dp", None),
        P(),
        P(("dp", "vocab"), None),
        P(("dp", "vocab"), None),
        P("vocab", None),
    )
    return jax.shard_map(
        shards, mesh=mesh, in_specs=placed, out_specs=P("dp", "vocab"), check_vma=False
    )
```
